256 devices in a mesh: ctx: 32 (over y, z), dp: 8 (over x, core).
Axes of the slice: x: 4, y: 4, z: 8, core: 2. Of those that a mesh axis runs over, the one named last changes fastest.
Arguments:
- queries: bfloat16 [4096, 4, 8192], P(('ctx', 'dp')), may hold values from -88 to 88
- new_kv: bfloat16 [4096, 4, 2048], P(('ctx', 'dp')), may hold values from -4 to 4
- kv_pages: bfloat16 [8192, 64, 2048], P(('ctx', 'dp')), may hold values from -6 to 6
- page_owner: int32 [8192, 1], P(('ctx', 'dp')), may hold values from 0 to 31; in each aligned block of 32 rows (0 to 31, 32 to 63, ...) at most 2 rows name the same one
- page_request: int32 [8192], P(('ctx', 'dp')), may hold values from 0 to 15
- page_fill: int32 [8192], P(('ctx', 'dp')), may hold values from 1 to 64
- prefix_kv: bfloat16 [512, 2048], P(('ctx', 'dp')), may hold values from -6 to 6
- prefix_use: int32 [4096], P(('ctx', 'dp')), may hold values 0 or 1
Outputs:
- attention: bfloat16 [4096, 4, 8192], P(('ctx', 'dp'))
The draws below stay inside these ranges and needn't reach their ends.
Inputs may be any that keep to these rules, and one draw needn't show every extreme that they name: `page_owner`: among one device's pages at most 2 name the same owner, and in some device's pages one owner is named exactly 2 times.
All inputs are finite; a program needn't handle non-finite values. No bound on the sum of `prefix_use` on one device may be relied on, other than what follows from the above.
Results may differ from the reference program's by a relative error of at most 0.0045.
Values may be sent and summed in bfloat16 or wider, within the bound.
A program may use at most 128 MiB of HBM per device.

```python
import math
import jax
import jax.numpy as jnp
import numpy as np
from jax import lax

QH = 64
KVH = 8
HD = 128
G = 8
PAGE = 64
STEPS = 4
REQ_DEV = 16
PAGES_DEV = 32
PREFIX = 512
MOST = 2
REQUESTS = 4096
PAGES = 8192
N_CTX = 32
N_DP = 8
DEVICES = 256


def shared_parts(key):
    shared_base = jnp.clip(jax.random.normal(jax.random.fold_in(key, 101), (REQUESTS, STEPS, KVH, HD), jnp.float32), -4.0, 4.0)
    return shared_base


def draw_new_kv(key, part):
    shared_base = shared_parts(key)
    key = jax.random.fold_in(key, 7)
    value_rows = jnp.clip(jax.random.normal(key, (REQUESTS, STEPS, KVH * HD), jnp.float32), -4.0, 4.0)
    key_rows = shared_base
    whole = jnp.concatenate([key_rows.reshape(REQUESTS, STEPS, KVH * HD), value_rows], axis=-1)
    return whole.astype(jnp.bfloat16)


def draw_queries(key, part):
    key = jax.random.fold_in(key, 9)
    whole = jnp.clip(jax.random.normal(key, (REQUESTS, STEPS, KVH, G, HD), jnp.float32), -4.0, 4.0)
    return whole.reshape(REQUESTS, STEPS, QH * HD).astype(jnp.bfloat16)


def touch_ends(values, stream_key, low, largest):
    spot = [jax.random.randint(jax.random.fold_in(stream_key, axis), (), 0, length) for axis, length in enumerate(values.shape)]
    main_axis = values.shape.index(max(values.shape))
    beside = spot[:main_axis] + [(spot[main_axis] + 1) % values.shape[main_axis]] + spot[main_axis + 1:]
    return values.at[tuple(spot)].set(low).at[tuple(beside)].set(largest)


def steps_of(key, shape, cuts, least, top_value):
    def one(position, parts):
        draws = jax.random.uniform(jax.random.fold_in(jax.random.fold_in(key, 6), position), (parts,), jnp.float32, least / len(cuts), top_value / len(cuts))
        return jnp.repeat(jnp.exp(draws), shape[position] // parts).reshape((-1,) + (1,) * (len(shape) - position - 1))

    loudness = one(*cuts[0])
    for cut in cuts[1:]:
        loudness = loudness * one(*cut)
    return loudness


def shared_out(stream_key, own, number, rows, number_of, top, limit, lean):
    order = jax.random.permutation(stream_key, number_of)
    packed, common = portions_of(number_of, rows * top, limit, lean, True), portions_of(number_of, rows * top, limit, lean, False)
    places = jnp.arange(number_of)

    def named(lengths, offset_by):
        used = int((lengths > 0).sum())
        fixed = max(1, used // 4)
        shifted = fixed + (places - fixed + offset_by * (used - fixed)) % max(1, number_of - fixed)
        return jnp.zeros((number_of,), jnp.int32).at[order[jnp.where(places < fixed, places, shifted)]].set(jnp.asarray(lengths, jnp.int32))

    lengths = jnp.where(number % 4 == 0, named(packed, number // 4), named(common, number - number // 4 - 1))
    mixed = jax.random.permutation(jax.random.fold_in(own, 3), number_of)
    donor, taker = mixed[0:number_of // 2 * 2:2], mixed[1:number_of // 2 * 2:2]
    margin = jnp.minimum(lengths[donor] - 1, limit - lengths[taker]) // 2
    margin = jnp.where((donor == order[0]) | (taker == order[0]) | (lengths[taker] == 0), 0, jnp.maximum(margin, 0))
    shifted = jax.random.randint(jax.random.fold_in(own, 4), (number_of // 2,), 0, 1 << 20) % (margin + 1)
    lengths = lengths.at[donor].add(-shifted).at[taker].add(shifted)
    labels = jnp.searchsorted(jnp.cumsum(lengths), jnp.arange(rows * top), side="right").astype(jnp.int32)
    table = labels.reshape(top, rows).T
    table = table[jax.random.permutation(jax.random.fold_in(own, 1), rows)]
    offset_by = jax.random.randint(jax.random.fold_in(own, 2), (rows, 1), 0, top)
    return jnp.take_along_axis(table, (jnp.arange(top)[None, :] + offset_by) % top, axis=1)


def portions_of(amount, total, most, lean, full):
    portions = [(1 << 20) // math.isqrt(rank ** lean) + 1 for rank in range(1, amount + 1)]
    largest = most if full else min(most, max(-(-total // amount), total * portions[0] // sum(portions)))
    least = 1 if total - largest >= amount - 1 else 0
    counts, spare = [largest] + [least] * (amount - 1), total - largest - least * (amount - 1)
    while spare > 0:
        movable = [i for i in range(1, amount) if counts[i] < largest] or [i for i in range(1, amount) if counts[i] < most]
        whole, budget = sum([portions[i] for i in movable]), spare
        for i in movable:
            addition = min(most - counts[i], max(1, budget * portions[i] // whole), spare)
            counts[i] = counts[i] + addition
            spare = spare - addition
    return np.array(counts)


def gaussian(rng, shape, scale, most, cuts=(), kind=jnp.bfloat16):
    level = steps_of(rng, shape, cuts, -0.22, 0.18) if cuts else 1.0
    array = jax.random.normal(rng, shape, jnp.float32) * scale * level
    return jnp.minimum(jnp.maximum(array, -most), most).astype(kind)


def setup_inputs(seed: int = 0) -> dict:
    streams_of = jax.random.split(jax.random.key(seed), 9)
    queries = draw_queries(jax.random.fold_in(streams_of[8], 71), 0)
    new_kv = draw_new_kv(jax.random.fold_in(streams_of[8], 71), 0)
    kv_pages = gaussian(streams_of[2], (PAGES, PAGE, 2 * KVH * HD), 1.0, 6.0, ((0, 256),))
    page_owner_keys = jax.random.split(jax.random.fold_in(streams_of[3], 1), PAGES // PAGES_DEV)
    page_owner_turns = jax.random.permutation(jax.random.fold_in(streams_of[3], 3), PAGES // PAGES_DEV)
    page_owner = jax.vmap(lambda own, number: shared_out(jax.random.fold_in(streams_of[3], 2), own, number, PAGES_DEV, N_CTX, 1, MOST, 2))(page_owner_keys, page_owner_turns).reshape((PAGES, 1))
    page_request = touch_ends(jax.random.randint(streams_of[4], (PAGES,), 0, REQ_DEV), jax.random.fold_in(streams_of[4], 1), 0, REQ_DEV - 1).astype(jnp.int32)
    page_fill = touch_ends(jax.random.randint(streams_of[5], (PAGES,), 1, PAGE + 1), jax.random.fold_in(streams_of[5], 1), 1, PAGE).astype(jnp.int32)
    prefix_kv = gaussian(streams_of[6], (PREFIX, 2 * KVH * HD), 1.0, 6.0, ((0, 256),))
    prefix_use = touch_ends((jax.random.randint(streams_of[7], (REQUESTS,), 0, 2) < 1).astype(jnp.int32), jax.random.fold_in(streams_of[7], 1), 0, 1)
    return {"queries": queries, "new_kv": new_kv, "kv_pages": kv_pages, "page_owner": page_owner, "page_request": page_request, "page_fill": page_fill, "prefix_kv": prefix_kv, "prefix_use": prefix_use}


masked_score = -1e+30

def group_parts(scores, visible, value_rows, form):
    scores = jnp.where(visible, scores, masked_score)
    highest = lax.optimization_barrier(jnp.max(scores, axis=-1))
    weights = jnp.where(visible, jnp.exp(scores - highest[..., None]), 0.0).astype(jnp.bfloat16)
    weights = lax.optimization_barrier(weights).astype(jnp.float32)
    totals = lax.optimization_barrier(jnp.sum(weights, axis=-1))
    output = jnp.einsum(form, weights, value_rows)
    return (highest, totals, output)

def reference(queries, new_kv, kv_pages, page_owner, page_request, page_fill, prefix_kv, prefix_use):
    scaling = 1.0 / math.sqrt(HD)
    width = KVH * HD
    block_of = jnp.arange(PAGES, dtype=jnp.int32) // PAGES_DEV
    target = (page_owner[:, 0] * N_DP + block_of % N_DP) * REQ_DEV + page_request
    target = target.astype(jnp.int32)

    def page_part(args):
        page_rows, target_rows, fill_rows = args
        query_rows = jnp.take(queries, target_rows, axis=0).astype(jnp.float32)
        query_rows = query_rows.reshape(PAGES_DEV, STEPS, KVH, G, HD)
        key_rows = page_rows[:, :, :width].astype(jnp.float32).reshape(PAGES_DEV, PAGE, KVH, HD)
        value_rows = page_rows[:, :, width:].astype(jnp.float32).reshape(PAGES_DEV, PAGE, KVH, HD)
        scores = jnp.einsum('sqkgd,stkd->skqgt', query_rows, key_rows) * scaling
        visible = (jnp.arange(PAGE, dtype=jnp.int32)[None, :] < fill_rows[:, None])[:, None, None, None, :]
        return group_parts(scores, visible, value_rows, 'skqgt,stkd->skqgd')
    blocks = (kv_pages.reshape(DEVICES, PAGES_DEV, PAGE, 2 * width), target.reshape(DEVICES, PAGES_DEV), page_fill.reshape(DEVICES, PAGES_DEV))
    page_max = lax.map(lambda args: page_part(args)[0], blocks)
    page_max = page_max.reshape(PAGES, KVH, STEPS, G)
    request_max = jnp.full((REQUESTS, KVH, STEPS, G), masked_score, jnp.float32).at[target].max(page_max)

    def accumulate(running, args):
        sums, outputs = running
        highest, totals, output = page_part(args)
        factor = jnp.exp(highest - request_max[args[1]])
        sums = sums.at[args[1]].add(factor * totals)
        outputs = outputs.at[args[1]].add(factor[..., None] * output)
        return ((sums, outputs), None)
    start = (jnp.zeros((REQUESTS, KVH, STEPS, G), jnp.float32), jnp.zeros((REQUESTS, KVH, STEPS, G, HD), jnp.float32))
    (page_sums, page_outputs), _ = lax.scan(accumulate, start, blocks)
    prefix_keys = prefix_kv[:, :width].astype(jnp.float32).reshape(PREFIX, KVH, HD)
    prefix_values = prefix_kv[:, width:].astype(jnp.float32).reshape(PREFIX, KVH, HD)
    causal = (jnp.arange(STEPS)[None, :] <= jnp.arange(STEPS)[:, None])[None, None, :, None, :]

    def finish(args):
        query_block, fresh_block, reading, max_block, sum_block, out_block = args
        query_rows = query_block.astype(jnp.float32).reshape(REQ_DEV, STEPS, KVH, G, HD)
        scores = jnp.einsum('rqkgd,tkd->rkqgt', query_rows, prefix_keys) * scaling
        everywhere = jnp.ones((1, 1, 1, 1, PREFIX), dtype=bool)
        prefix_max, prefix_sum, prefix_out = group_parts(scores, everywhere, prefix_values, 'rkqgt,tkd->rkqgd')
        reads = (reading > 0)[:, None, None, None]
        prefix_max = jnp.where(reads, prefix_max, masked_score)
        prefix_sum = jnp.where(reads, prefix_sum, 0.0)
        prefix_out = jnp.where(reads[..., None], prefix_out, 0.0)
        fresh_keys = fresh_block[:, :, :width].astype(jnp.float32).reshape(REQ_DEV, STEPS, KVH, HD)
        fresh_values = fresh_block[:, :, width:].astype(jnp.float32).reshape(REQ_DEV, STEPS, KVH, HD)
        scores = jnp.einsum('rqkgd,rtkd->rkqgt', query_rows, fresh_keys) * scaling
        fresh_max, fresh_sum, fresh_out = group_parts(scores, causal, fresh_values, 'rkqgt,rtkd->rkqgd')
        overall = jnp.maximum(jnp.maximum(max_block, prefix_max), fresh_max)
        page_factor = jnp.exp(max_block - overall)
        prefix_factor = jnp.exp(prefix_max - overall)
        fresh_factor = jnp.exp(fresh_max - overall)
        totals = page_factor * sum_block + prefix_factor * prefix_sum + fresh_factor * fresh_sum
        output = page_factor[..., None] * out_block + prefix_factor[..., None] * prefix_out + fresh_factor[..., None] * fresh_out
        output = output / totals[..., None]
        output = jnp.transpose(output, (0, 2, 1, 3, 4)).reshape(REQ_DEV, STEPS, QH * HD)
        return output.astype(jnp.bfloat16)
    final = lax.map(finish, (queries.reshape(DEVICES, REQ_DEV, STEPS, QH * HD), new_kv.reshape(DEVICES, REQ_DEV, STEPS, 2 * width), prefix_use.reshape(DEVICES, REQ_DEV), request_max.reshape(DEVICES, REQ_DEV, KVH, STEPS, G), page_sums.reshape(DEVICES, REQ_DEV, KVH, STEPS, G), page_outputs.reshape(DEVICES, REQ_DEV, KVH, STEPS, G, HD)))
    return final.reshape(REQUESTS, STEPS, QH * HD)
```

```python
import functools
import math

import jax
import jax.numpy as jnp
from jax import lax
from jax.experimental import pallas as pl
from jax.experimental.pallas import tpu as pltpu
from jax.sharding import PartitionSpec as P

KVH = 8
HD = 128
G = 8
LOW = -1e30
NY, NZ = 4, 8
NCTX = NY * NZ
NDP = 8
MESH = pl.DeviceIdType.MESH
SCALE = 1.0 / math.sqrt(HD)


def lane_head(rows):
    return lax.broadcasted_iota(jnp.int32, (rows, 128), 1) // 32


def spread(block, rows):
    head = lane_head(rows)
    zero = jnp.zeros_like(block)
    return jnp.concatenate([jnp.where(head == k, block, zero) for k in range(4)], axis=0)


def scores_half(keys, qt):
    s = lax.dot_general(
        keys, spread(qt, HD), (((1,), (0,)), ((), ())), preferred_element_type=jnp.float32
    )
    return s * SCALE


def values_half(values, w):
    stacked = jnp.concatenate(values, axis=0)
    return lax.dot_general(
        stacked,
        spread(w, w.shape[0]),
        (((0,), (0,)), ((), ())),
        preferred_element_type=jnp.float32,
    )


def group_half(keys, values, qt, visible):
    s = scores_half(keys, qt)
    if visible is not None:
        s = jnp.where(visible, s, LOW)
    m = jnp.max(s, axis=0, keepdims=True)
    w = jnp.exp(s - m)
    if visible is not None:
        w = jnp.where(visible, w, 0.0)
    w = w.astype(jnp.bfloat16)
    l = jnp.sum(w.astype(jnp.float32), axis=0, keepdims=True)
    return m, l, values_half(values, w)


def kernel(
    req, page_of, fill_of, use,
    qt_ref, pages_ref, fresh_ref, prefix_ref,
    out_ref,
    sendq, recvq, sendp, recvp, sendl, recvl,
    acc, big, tot, pre1, pre2, pre3, pre4,
    sq_sem, rq_sem, sp_sem, rp_sem, sl_sem, rl_sem, s1_sem, r1_sem, s2_sem, r2_sem, loc_sem,
):
    me = lax.axis_index("ctx")
    col = lax.axis_index("dp")
    y, z = me // NZ, me % NZ

    def ahead(i):
        return ((y + i // NZ) % NY) * NZ + (z + i % NZ) % NZ

    def behind(i):
        return ((y + NY - i // NZ) % NY) * NZ + (z + NZ - i % NZ) % NZ

    barrier = pltpu.get_barrier_semaphore()

    def greet(i, c):
        pl.semaphore_signal(barrier, inc=1, device_id={"ctx": ahead(i)}, device_id_type=MESH)
        return c

    lax.fori_loop(1, NCTX, greet, 0)

    def greet_dp(i, c):
        pl.semaphore_signal(barrier, inc=1, device_id={"dp": (col + i) % NDP}, device_id_type=MESH)
        return c

    lax.fori_loop(1, NDP, greet_dp, 0)
    pl.semaphore_wait(barrier, NCTX + NDP - 2)

    def pre_copy(i):
        return pltpu.make_async_remote_copy(
            src_ref=prefix_ref, dst_ref=pre1.at[i], send_sem=s1_sem.at[i], recv_sem=r1_sem.at[i],
            device_id={"ctx": ahead(i)}, device_id_type=MESH)

    def pre_start(i, c):
        pre_copy(i).start()
        return c

    lax.fori_loop(1, NCTX, pre_start, 0)
    pre1[0] = prefix_ref[...]

    def q_copy(i):
        return pltpu.make_async_remote_copy(
            src_ref=sendq.at[i], dst_ref=recvq.at[i], send_sem=sq_sem.at[i], recv_sem=rq_sem.at[i],
            device_id={"ctx": ahead(i)}, device_id_type=MESH)

    def gather(i, d):
        for s in range(2):
            r = jnp.maximum(req[2 * d + s], 0)
            sendq[i, s] = qt_ref[r]

    def q_start(i, c):
        gather(i, ahead(i))
        q_copy(i).start()
        return c

    lax.fori_loop(1, NCTX, q_start, 0)
    gather(0, me)

    def pre_wait(i, c):
        pre_copy(i).wait()
        return c

    lax.fori_loop(1, NCTX, pre_wait, 0)

    def pre2_copy(i):
        return pltpu.make_async_remote_copy(
            src_ref=pre1, dst_ref=pre2.at[i], send_sem=s2_sem.at[i], recv_sem=r2_sem.at[i],
            device_id={"dp": (col + i) % NDP}, device_id_type=MESH)

    def pre2_start(i, c):
        pre2_copy(i).start()
        return c

    lax.fori_loop(1, NDP, pre2_start, 0)
    pre2[0] = pre1[...]

    def fresh(r, c):
        t = lax.broadcasted_iota(jnp.int32, (16, 128), 0)
        step = lax.broadcasted_iota(jnp.int32, (16, 128), 1) % 4
        visible = t <= step
        for h in range(2):
            ln = pl.ds(h * 128, 128)
            keys = fresh_ref[r, :, pl.ds(h * 512, 512)]
            values = [fresh_ref[r, :, pl.ds(1024 + (4 * h + k) * 128, 128)] for k in range(4)]
            m, l, o = group_half(keys, values, qt_ref[r, :, ln], visible)
            big[r, :, ln] = m
            tot[r, :, ln] = l
            acc[r, :, ln] = o
        return c

    lax.fori_loop(0, 16, fresh, 0)

    def attend(src, i, o, dst_o, dst_l):
        for s in range(2):
            p = page_of[2 * o + s]
            f = fill_of[2 * o + s]
            visible = lax.broadcasted_iota(jnp.int32, (64, 128), 0) < f
            for h in range(2):
                ln = pl.ds(h * 128, 128)
                keys = pages_ref[p, :, pl.ds(h * 512, 512)]
                values = [pages_ref[p, :, pl.ds(1024 + (4 * h + k) * 128, 128)] for k in range(4)]
                m, l, out = group_half(keys, values, src[i, s, :, ln], visible)
                dst_o[i, s, :, ln] = (out * (1.0 / l)).astype(jnp.bfloat16)
                dst_l[i, pl.ds(s, 1), ln] = m + jnp.log(l)

    attend(sendq, 0, me, recvp, recvl)

    def p_copy(i):
        return pltpu.make_async_remote_copy(
            src_ref=sendp.at[i], dst_ref=recvp.at[i], send_sem=sp_sem.at[i], recv_sem=rp_sem.at[i],
            device_id={"ctx": behind(i)}, device_id_type=MESH)

    def l_copy(i):
        return pltpu.make_async_remote_copy(
            src_ref=sendl.at[i], dst_ref=recvl.at[i], send_sem=sl_sem.at[i], recv_sem=rl_sem.at[i],
            device_id={"ctx": behind(i)}, device_id_type=MESH)

    def answer(i, c):
        q_copy(i).wait()
        attend(recvq, i, behind(i), sendp, sendl)
        l_copy(i).start()
        p_copy(i).start()
        return c

    lax.fori_loop(1, NCTX, answer, 0)

    def pre2_wait(i, c):
        pre2_copy(i).wait()
        return c

    lax.fori_loop(1, NDP, pre2_wait, 0)

    def widen(i, c):
        pre3[...] = pre2[i].astype(jnp.float32).reshape(NCTX * 32, 128)
        for ch in range(16):
            pre4[ch, pl.ds(pl.multiple_of(i * 2 * NCTX, 2 * NCTX), 2 * NCTX), :] = pre3[pl.ds(ch, 2 * NCTX, stride=16), :].astype(jnp.bfloat16)
        return c

    lax.fori_loop(0, NDP, widen, 0)

    def prefix(r, c):
        u = use[r] > 0
        for h in range(2):
            ln = pl.ds(h * 128, 128)
            q = qt_ref[r, :, ln]
            head = lane_head(HD)
            s = jnp.zeros((2 * NCTX * NDP, 128), jnp.float32)
            for k in range(4):
                s = s + lax.dot_general(pre4[4 * h + k], jnp.where(head == k, q, jnp.zeros_like(q)),
                    (((1,), (0,)), ((), ())), preferred_element_type=jnp.float32)
            s = s * SCALE
            m = jnp.max(s, axis=0, keepdims=True)
            w = jnp.exp(s - m).astype(jnp.bfloat16)
            l = jnp.sum(w.astype(jnp.float32), axis=0, keepdims=True)
            o = values_half([pre4[8 + 4 * h + k] for k in range(4)], w)
            m = jnp.where(u, m, LOW)
            l = jnp.where(u, l, 0.0)
            o = jnp.where(u, o, 0.0)
            old = big[r, :, ln]
            new = jnp.maximum(old, m)
            a, b = jnp.exp(old - new), jnp.exp(m - new)
            big[r, :, ln] = new
            tot[r, :, ln] = a * tot[r, :, ln] + b * l
            acc[r, :, ln] = a * acc[r, :, ln] + b * o
        return c

    lax.fori_loop(0, 16, prefix, 0)

    def merge(i, d):
        r0, r1 = req[2 * d], req[2 * d + 1]

        def one(r, c):
            l0 = jnp.where(r0 == r, recvl[i, 0:1, :], LOW)
            l1 = jnp.where(r1 == r, recvl[i, 1:2, :], LOW)
            old = big[r]
            new = jnp.maximum(old, jnp.maximum(l0, l1))
            a, b0, b1 = jnp.exp(old - new), jnp.exp(l0 - new), jnp.exp(l1 - new)
            big[r] = new
            tot[r] = a * tot[r] + b0 + b1
            acc[r] = a * acc[r] + b0 * recvp[i, 0].astype(jnp.float32) + b1 * recvp[i, 1].astype(jnp.float32)
            return c

        lax.fori_loop(0, 16, one, 0)

    merge(0, me)

    def take(i, c):
        l_copy(i).wait()
        p_copy(i).wait()
        merge(i, ahead(i))
        return c

    lax.fori_loop(1, NCTX, take, 0)

    def finish(r, c):
        out_ref[r] = (acc[r] * (1.0 / tot[r])).astype(jnp.bfloat16)
        return c

    lax.fori_loop(0, 16, finish, 0)


def body(queries, new_kv, kv_pages, page_owner, page_request, page_fill, prefix_kv, prefix_use):
    pages_dev, page_len, channels = kv_pages.shape
    request_count, step_count, query_width = queries.shape
    slots = 2 * NCTX
    owners = page_owner[:, 0]
    owner_hot = (owners[:, None] == jnp.arange(NCTX, dtype=jnp.int32)[None, :]).astype(jnp.int32)
    earlier = jnp.cumsum(owner_hot, axis=0) - owner_hot
    position = jnp.sum(earlier * owner_hot, axis=1)
    slot_of_page = owners * 2 + position
    matches = (slot_of_page[None, :] == jnp.arange(slots, dtype=jnp.int32)[:, None]).astype(jnp.int32)
    present = jnp.sum(matches, axis=1)
    page_of = jnp.sum(matches * jnp.arange(pages_dev, dtype=jnp.int32)[None, :], axis=1)
    send_request = jnp.where(present > 0, jnp.sum(matches * page_request[None, :], axis=1), -1)
    fill_of = jnp.maximum(jnp.sum(matches * page_fill[None, :], axis=1), 1)
    req = lax.all_to_all(send_request.reshape(NCTX, 2), "ctx", split_axis=0, concat_axis=0, tiled=True).reshape(slots)

    qt = queries.reshape(request_count, step_count, KVH * G, HD).transpose(0, 3, 2, 1).reshape(request_count, HD, 256)
    fresh = jnp.pad(new_kv, ((0, 0), (0, 12), (0, 0)))
    prefix = prefix_kv.reshape(32, 128)

    smem = pl.BlockSpec(memory_space=pltpu.SMEM)
    vmem = pl.BlockSpec(memory_space=pltpu.VMEM)
    dma = pltpu.SemaphoreType.DMA
    out = pl.pallas_call(
        kernel,
        out_shape=jax.ShapeDtypeStruct((request_count, HD, 256), jnp.bfloat16),
        in_specs=[smem] * 4 + [vmem] * 4,
        out_specs=vmem,
        scratch_shapes=[
            pltpu.VMEM((NCTX, 2, HD, 256), jnp.bfloat16),
            pltpu.VMEM((NCTX, 2, HD, 256), jnp.bfloat16),
            pltpu.VMEM((NCTX, 2, HD, 256), jnp.bfloat16),
            pltpu.VMEM((NCTX, 2, HD, 256), jnp.bfloat16),
            pltpu.VMEM((NCTX, 2, 256), jnp.float32),
            pltpu.VMEM((NCTX, 2, 256), jnp.float32),
            pltpu.VMEM((16, HD, 256), jnp.float32),
            pltpu.VMEM((16, 1, 256), jnp.float32),
            pltpu.VMEM((16, 1, 256), jnp.float32),
            pltpu.VMEM((NCTX, 32, 128), jnp.bfloat16),
            pltpu.VMEM((NDP, NCTX, 32, 128), jnp.bfloat16),
            pltpu.VMEM((NCTX * 32, 128), jnp.float32),
            pltpu.VMEM((16, 2 * NCTX * NDP, 128), jnp.bfloat16),
            dma((NCTX,)), dma((NCTX,)), dma((NCTX,)), dma((NCTX,)), dma((NCTX,)), dma((NCTX,)),
            dma((NCTX,)), dma((NCTX,)), dma((NDP,)), dma((NDP,)), dma,
        ],
        compiler_params=pltpu.CompilerParams(
            collective_id=0, has_side_effects=True, vmem_limit_bytes=60 * 2**20
        ),
    )(req, page_of, fill_of, prefix_use, qt, kv_pages, fresh, prefix)
    out = out.reshape(request_count, HD, KVH * G, step_count).transpose(0, 3, 2, 1)
    return out.reshape(request_count, step_count, query_width)


def solution(mesh):
    placed = (
        P(("ctx", "dp"), None, None),
        P(("ctx", "dp"), None, None),
        P(("ctx", "dp"), None, None),
        P(("ctx", "dp"), None),
        P(("ctx", "dp")),
        P(("ctx", "dp")),
        P(("ctx", "dp"), None),
        P(("ctx", "dp")),
    )
    return jax.shard_map(
        body, mesh=mesh, in_specs=placed, out_specs=P(("ctx", "dp"), None, None), check_vma=False
    )
```

```python
import functools
import math

import jax
import jax.numpy as jnp
from jax import lax
from jax.experimental import pallas as pl
from jax.experimental.pallas import tpu as pltpu
from jax.sharding import PartitionSpec as P

KVH = 8
HD = 128
G = 8
LOW = -1e30
NY, NZ = 4, 8
NCTX = NY * NZ
NDP = 8
EARLY = 32
RELAY = 12
TAKEN = 20
MESH = pl.DeviceIdType.MESH
SCALE = 1.0 / math.sqrt(HD)


def meta_kernel(owner, request, fill, table, own, level, mine, tally, sa, ra, sb, rb):
    me = lax.axis_index("ctx")
    col = lax.axis_index("dp")
    y, z = me // NZ, me % NZ

    def ahead(i):
        return ((y + i // NZ) % NY) * NZ + (z + i % NZ) % NZ

    barrier = pltpu.get_barrier_semaphore()
    for i in range(1, NCTX):
        pl.semaphore_signal(barrier, inc=1, device_id={"ctx": ahead(i)}, device_id_type=MESH)
    for i in range(1, NDP):
        pl.semaphore_signal(barrier, inc=1, device_id={"dp": (col + i) % NDP}, device_id_type=MESH)

    lane = lax.broadcasted_iota(jnp.int32, (8, 128), 1)
    count = jnp.zeros((8, 128), jnp.int32)
    r0 = jnp.full((8, 128), -1, jnp.int32)
    r1, p0, p1, f0, f1 = r0, count, count, count + 1, count + 1
    for p in range(owner.shape[0]):
        hit = lane == owner[p, 0]
        first, second = hit & (count == 0), hit & (count == 1)
        r0, r1 = jnp.where(first, request[p], r0), jnp.where(second, request[p], r1)
        p0, p1 = jnp.where(first, p, p0), jnp.where(second, p, p1)
        f0, f1 = jnp.where(first, fill[p], f0), jnp.where(second, fill[p], f1)
        count = count + hit.astype(jnp.int32)
    own[0:1, :] = p0[0:1]
    own[1:2, :] = p1[0:1]
    own[2:3, :] = f0[0:1]
    own[3:4, :] = f1[0:1]
    extra = jnp.where(count == 2, 1, 0)
    whole = extra
    for k in range(1, NY):
        whole = whole + pltpu.roll(extra, k * NZ, 1)
    most = jnp.max(whole, axis=1, keepdims=True)
    tally[0] = jnp.broadcast_to(most, (8, 128))

    pl.semaphore_wait(barrier, NCTX + NDP - 2)

    def tally_copy(i):
        return pltpu.make_async_remote_copy(
            src_ref=tally.at[0], dst_ref=tally.at[i], send_sem=sa.at[i], recv_sem=ra.at[i],
            device_id={"dp": (col + i) % NDP}, device_id_type=MESH)

    for i in range(1, NDP):
        tally_copy(i).start()
    for i in range(1, NDP):
        tally_copy(i).wait()
    most = tally[0]
    for i in range(1, NDP):
        most = jnp.maximum(most, tally[i])
    row = jnp.where(lane < NCTX, r0, jnp.where(lane < 2 * NCTX, pltpu.roll(r1, NCTX, 1), most))
    mine[0] = row[0:1]
    table[pl.ds(me, 1)] = row[0:1].reshape(1, 1, 128)

    def row_copy(i):
        return pltpu.make_async_remote_copy(
            src_ref=mine.at[0], dst_ref=table.at[me], send_sem=sb.at[i], recv_sem=rb.at[i],
            device_id={"ctx": ahead(i)}, device_id_type=MESH)

    for i in range(1, NCTX):
        row_copy(i).start()
    for i in range(1, NCTX):
        row_copy(i).wait()
    far = table[0]
    for h in range(1, NCTX):
        far = jnp.maximum(far, table[h])
    need = jnp.max(jnp.where(lax.broadcasted_iota(jnp.int32, (1, 128), 1) >= 2 * NCTX, far, 0), axis=1, keepdims=True)
    level[...] = jnp.broadcast_to(jnp.where(need <= 1, 0, jnp.where(need <= 2, 1, 2)), (1, 128))


def lane_head(rows):
    return lax.broadcasted_iota(jnp.int32, (rows, 128), 1) // 32


def spread(block, rows):
    head = lane_head(rows)
    zero = jnp.zeros_like(block)
    return jnp.concatenate([jnp.where(head == k, block, zero) for k in range(4)], axis=0)


def values_half(values, w):
    stacked = jnp.concatenate(values, axis=0)
    return lax.dot_general(
        stacked, spread(w, w.shape[0]), (((0,), (0,)), ((), ())), preferred_element_type=jnp.float32
    )


def group_half(keys, values, qt, visible):
    s = lax.dot_general(
        keys, spread(qt, HD), (((1,), (0,)), ((), ())), preferred_element_type=jnp.float32
    ) * SCALE
    s = jnp.where(visible, s, LOW)
    m = jnp.max(s, axis=0, keepdims=True)
    w = jnp.where(visible, jnp.exp(s - m), 0.0).astype(jnp.bfloat16)
    l = jnp.sum(w.astype(jnp.float32), axis=0, keepdims=True)
    return m, l, values_half(values, w)


def kernel(
    cap, table, own, use,
    qt_ref, pages_hbm, fresh_ref, prefix_ref,
    out_ref,
    pages_ref, sq, rq, sp, rp, sl, rl,
    sq2, rq2, spk, rpk, sp2, rp2, sl2, rl2, su, ru, sul, rul,
    acc, big, tot, pre0, pre1, pre2, pre3, pre4,
    sq_s, rq_s, sp_s, rp_s, sl_s, rl_s,
    sq2_s, rq2_s, spk_s, rpk_s, sp2_s, rp2_s, sl2_s, rl2_s, su_s, ru_s, sul_s, rul_s,
    a_s, a_r, b_s, b_r, c_s, c_r, page_s,
):
    me = lax.axis_index("ctx")
    col = lax.axis_index("dp")
    y, z = me // NZ, me % NZ

    page_load = pltpu.make_async_copy(pages_hbm, pages_ref, page_s)
    page_load.start()

    def at(a, b):
        return (a % NY) * NZ + b % NZ

    def ahead(i):
        return at(y + i // NZ, z + i % NZ)

    def behind(i):
        return at(y + NY - i // NZ, z + NZ - i % NZ)

    def remote(src, dst, send, recv, ctx):
        return pltpu.make_async_remote_copy(
            src_ref=src, dst_ref=dst, send_sem=send, recv_sem=recv,
            device_id={"ctx": ctx}, device_id_type=MESH)

    def loop(lo, hi, f):
        def step(i, c):
            f(i)
            return c

        lax.fori_loop(lo, hi, step, 0)

    barrier = pltpu.get_barrier_semaphore()
    loop(1, NCTX, lambda i: pl.semaphore_signal(barrier, inc=1, device_id={"ctx": ahead(i)}, device_id_type=MESH))
    loop(1, NDP, lambda i: pl.semaphore_signal(barrier, inc=1, device_id={"dp": (col + i) % NDP}, device_id_type=MESH))
    pl.semaphore_wait(barrier, NCTX + NDP - 2)

    def pre_z(i):
        return remote(prefix_ref, pre0.at[i], a_s.at[i], a_r.at[i], at(y, z + i))

    def pre_y(i):
        return remote(pre0, pre1.at[i], b_s.at[i], b_r.at[i], at(y + i, z))

    def pre_dp(i):
        return pltpu.make_async_remote_copy(
            src_ref=pre1, dst_ref=pre2.at[i], send_sem=c_s.at[i], recv_sem=c_r.at[i],
            device_id={"dp": (col + i) % NDP}, device_id_type=MESH)

    loop(1, NZ, lambda i: pre_z(i).start())
    pre0[0] = prefix_ref[...]

    def q2_copy(i):
        return remote(sq2.at[i], rq2.at[i], sq2_s.at[i], rq2_s.at[i], at(y + i, z))

    def wanted(h, second):
        return qt_ref[jnp.maximum(table[h, 0, second * NCTX + me], 0)]

    def relay_queries(i):
        def one(zh):
            sq2[i, zh] = wanted(at(y + i, zh), 1)

        loop(0, NZ, one)
        q2_copy(i).start()

    def q_copy(i):
        return remote(sq.at[i], rq.at[i], sq_s.at[i], rq_s.at[i], ahead(i))

    def send_queries(i):
        sq[i] = wanted(ahead(i), 0)
        q_copy(i).start()

    loop(1, NY, relay_queries)
    loop(1, NCTX, send_queries)
    rq[0] = wanted(me, 0)

    def own_relay(zh):
        rq2[0, zh] = wanted(at(y, zh), 1)

    loop(0, NZ, own_relay)

    loop(1, NZ, lambda i: pre_z(i).wait())
    loop(1, NY, lambda i: pre_y(i).start())
    pre1[0] = pre0[...]

    t = lax.broadcasted_iota(jnp.int32, (16, 128), 0)
    causal = t <= lax.broadcasted_iota(jnp.int32, (16, 128), 1) % 4

    def fresh(r):
        for h in range(2):
            ln = pl.ds(h * 128, 128)
            keys = fresh_ref[r, :, pl.ds(h * 512, 512)]
            values = [fresh_ref[r, :, pl.ds(1024 + (4 * h + k) * 128, 128)] for k in range(4)]
            m, l, o = group_half(keys, values, qt_ref[r, :, ln], causal)
            big[r, :, ln] = m
            tot[r, :, ln] = l
            acc[r, :, ln] = o

    loop(0, 16, fresh)

    loop(1, NY, lambda i: pre_y(i).wait())
    loop(1, NDP, lambda i: pre_dp(i).start())
    pre2[0] = pre1[...]

    page_load.wait()

    def attend(q, p, f, put_o, put_l):
        visible = lax.broadcasted_iota(jnp.int32, (64, 128), 0) < f
        for h in range(2):
            ln = pl.ds(h * 128, 128)
            keys = pages_ref[p, :, pl.ds(h * 512, 512)]
            values = [pages_ref[p, :, pl.ds(1024 + (4 * h + k) * 128, 128)] for k in range(4)]
            m, l, out = group_half(keys, values, q[:, ln], visible)
            put_o[:, ln] = (out * (1.0 / l)).astype(jnp.bfloat16)
            put_l[:, ln] = m + jnp.log(l)

    def p_copy(i):
        return remote(sp.at[i], rp.at[i], sp_s.at[i], rp_s.at[i], behind(i))

    def l_copy(i):
        return remote(sl.at[i], rl.at[i], sl_s.at[i], rl_s.at[i], behind(i))

    def answer(i):
        q_copy(i).wait()
        o = behind(i)
        attend(rq.at[i], own[0, o], own[2, o], sp.at[i], sl.at[i])
        l_copy(i).start()
        p_copy(i).start()

    attend(rq.at[0], own[0, me], own[2, me], rp.at[0], rl.at[0])

    def in_use(h, plane):
        return [(table[h, 0, NCTX + k * NZ + plane] >= 0).astype(jnp.int32) for k in range(NY)]

    def nth(flags, j):
        place, seen = 0, 0
        for k in range(NY):
            place = jnp.where((flags[k] == 1) & (seen == j), k, place)
            seen = seen + flags[k]
        return place

    def pack_copy(d):
        return remote(spk.at[d], rpk.at[d], spk_s.at[d], rpk_s.at[d], at(y, z + d))

    def pack(d, dst):
        zh = (z + d) % NZ
        flags = in_use(at(y, zh), z)
        for j in range(cap):
            dst[d, j] = rq2[(y + NY - nth(flags, j)) % NY, zh]

    def pack_send(d):
        pack(d, spk)
        pack_copy(d).start()

    def p2_copy(d):
        return remote(sp2.at[d], rp2.at[d], sp2_s.at[d], rp2_s.at[d], at(y, z + NZ - d))

    def l2_copy(d):
        return remote(sl2.at[d], rl2.at[d], sl2_s.at[d], rl2_s.at[d], at(y, z + NZ - d))

    def attend2(d, dst_o, dst_l):
        plane = (z + NZ - d) % NZ
        flags = in_use(me, plane)
        for j in range(cap):
            o = nth(flags, j) * NZ + plane
            attend(rpk.at[d, j], own[1, o], own[3, o], dst_o.at[d, j], dst_l.at[d, j])

    def answer2(d):
        pack_copy(d).wait()
        attend2(d, sp2, sl2)
        l2_copy(d).start()
        p2_copy(d).start()

    def u_copy(i, zh):
        return remote(su.at[i, zh], ru.at[i, zh], su_s.at[i, zh], ru_s.at[i, zh], at(y + i, z))

    def ul_copy(i, zh):
        return remote(sul.at[i, zh], rul.at[i, zh], sul_s.at[i, zh], rul_s.at[i, zh], at(y + i, z))

    def hand_on(d):
        zh = (z + d) % NZ
        flags = in_use(at(y, zh), z)
        for i in range(NY):
            k = (y + i) % NY
            before = 0
            for k2 in range(NY):
                before = before + jnp.where(k2 < k, flags[k2], 0)
            o, l = rp2[d, 0], rl2[d, 0]
            for j in range(1, cap):
                o, l = jnp.where(before >= j, rp2[d, j], o), jnp.where(before >= j, rl2[d, j], l)
            if i == 0:
                ru[0, zh] = o
                rul[0, zh] = l
            else:
                su[i, zh] = o
                sul[i, zh] = l
                ul_copy(i, zh).start()
                u_copy(i, zh).start()

    loop(1, RELAY, answer)
    loop(1, NY, lambda i: q2_copy(i).wait())
    loop(1, NZ, pack_send)
    pack(0, rpk)
    attend2(0, rp2, rl2)
    loop(RELAY, EARLY, answer)
    loop(1, NZ, answer2)
    loop(EARLY, NCTX, answer)

    loop(1, NDP, lambda i: pre_dp(i).wait())

    def widen(i):
        pre3[...] = pre2[i].astype(jnp.float32).reshape(NCTX * 32, 128)
        for ch in range(16):
            pre4[ch, pl.ds(pl.multiple_of(i * 2 * NCTX, 2 * NCTX), 2 * NCTX), :] = pre3[
                pl.ds(ch, 2 * NCTX, stride=16), :].astype(jnp.bfloat16)

    loop(0, NDP, widen)

    def prefix(r):
        u = use[r] > 0
        for h in range(2):
            ln = pl.ds(h * 128, 128)
            q = qt_ref[r, :, ln]
            head = lane_head(HD)
            s = jnp.zeros((2 * NCTX * NDP, 128), jnp.float32)
            for k in range(4):
                s = s + lax.dot_general(
                    pre4[4 * h + k], jnp.where(head == k, q, jnp.zeros_like(q)),
                    (((1,), (0,)), ((), ())), preferred_element_type=jnp.float32)
            s = s * SCALE
            m = jnp.max(s, axis=0, keepdims=True)
            w = jnp.exp(s - m).astype(jnp.bfloat16)
            l = jnp.sum(w.astype(jnp.float32), axis=0, keepdims=True)
            o = values_half([pre4[8 + 4 * h + k] for k in range(4)], w)
            m = jnp.where(u, m, LOW)
            l = jnp.where(u, l, 0.0)
            o = jnp.where(u, o, 0.0)
            old = big[r, :, ln]
            new = jnp.maximum(old, m)
            a, b = jnp.exp(old - new), jnp.exp(m - new)
            big[r, :, ln] = new
            tot[r, :, ln] = a * tot[r, :, ln] + b * l
            acc[r, :, ln] = a * acc[r, :, ln] + b * o

    loop(0, 16, prefix)

    def merge(items):
        def one(r):
            ls = [jnp.where(q == r, l[...], LOW) for q, l, _ in items]
            old = big[r]
            new = functools.reduce(jnp.maximum, ls, old)
            a = jnp.exp(old - new)
            bs = [jnp.exp(l - new) for l in ls]
            big[r] = new
            tot[r] = functools.reduce(lambda x, b: x + b, bs, a * tot[r])
            more = a * acc[r]
            for b, (_, _, o) in zip(bs, items):
                more = more + b * o[...].astype(jnp.float32)
            acc[r] = more

        loop(0, 16, one)

    def take(k):
        def arrive(i):
            l_copy(i).wait()
            p_copy(i).wait()

        loop(4 * k, 4 * k + 4, arrive)
        merge([(table[ahead(4 * k + n), 0, me], rl.at[4 * k + n], rp.at[4 * k + n]) for n in range(4)])

    def arrive(i):
        l_copy(i).wait()
        p_copy(i).wait()

    loop(1, 4, arrive)
    merge([(table[ahead(n), 0, me], rl.at[n], rp.at[n]) for n in range(4)])
    loop(1, TAKEN // 4, take)

    def relay_back(d):
        l2_copy(d).wait()
        p2_copy(d).wait()
        hand_on(d)

    hand_on(0)
    loop(1, NZ, relay_back)
    loop(TAKEN // 4, NCTX // 4, take)

    def merge_second(i, zh):
        n = min(4, NZ)
        hs = [zh + j for j in range(n)]
        merge([(table[at(y + NY - i, h), 0, NCTX + me], rul.at[i, h], ru.at[i, h]) for h in hs])

    def take_second(i):
        def arrive2(zh):
            ul_copy(i, zh).wait()
            u_copy(i, zh).wait()

        loop(0, NZ, arrive2)
        loop(0, max(1, NZ // 4), lambda k: merge_second(i, 4 * k))

    loop(0, max(1, NZ // 4), lambda k: merge_second(0, 4 * k))
    loop(1, NY, take_second)

    def finish(r):
        out_ref[r] = (acc[r] * (1.0 / tot[r])).astype(jnp.bfloat16)

    loop(0, 16, finish)


def attend_all(cap, table, own, use, qt, pages, fresh, prefix):
    smem = pl.BlockSpec(memory_space=pltpu.SMEM)
    vmem = pl.BlockSpec(memory_space=pltpu.VMEM)
    dma = pltpu.SemaphoreType.DMA

    def rows(*lead):
        return pltpu.VMEM(lead + (HD, 256), jnp.bfloat16)

    def stats(*lead):
        return pltpu.VMEM(lead + (1, 256), jnp.float32)

    return pl.pallas_call(
        functools.partial(kernel, cap),
        out_shape=jax.ShapeDtypeStruct(qt.shape, jnp.bfloat16),
        in_specs=[smem] * 3 + [vmem, pl.BlockSpec(memory_space=pl.ANY), vmem, vmem],
        out_specs=vmem,
        scratch_shapes=[
            pltpu.VMEM(pages.shape, jnp.bfloat16),
            rows(NCTX), rows(NCTX), rows(NCTX), rows(NCTX), stats(NCTX), stats(NCTX),
            rows(NY, NZ), rows(NY, NZ), rows(NZ, cap), rows(NZ, cap), rows(NZ, cap), rows(NZ, cap),
            stats(NZ, cap), stats(NZ, cap), rows(NY, NZ), rows(NY, NZ), stats(NY, NZ), stats(NY, NZ),
            pltpu.VMEM((16, HD, 256), jnp.float32), stats(16), stats(16),
            pltpu.VMEM((NZ, 32, 128), jnp.bfloat16),
            pltpu.VMEM((NY, NZ, 32, 128), jnp.bfloat16),
            pltpu.VMEM((NDP, NY, NZ, 32, 128), jnp.bfloat16),
            pltpu.VMEM((NCTX * 32, 128), jnp.float32),
            pltpu.VMEM((16, 2 * NCTX * NDP, 128), jnp.bfloat16),
            dma((NCTX,)), dma((NCTX,)), dma((NCTX,)), dma((NCTX,)), dma((NCTX,)), dma((NCTX,)),
            dma((NY,)), dma((NY,)), dma((NZ,)), dma((NZ,)), dma((NZ,)), dma((NZ,)), dma((NZ,)), dma((NZ,)),
            dma((NY, NZ)), dma((NY, NZ)), dma((NY, NZ)), dma((NY, NZ)),
            dma((NZ,)), dma((NZ,)), dma((NY,)), dma((NY,)), dma((NDP,)), dma((NDP,)), dma,
        ],
        compiler_params=pltpu.CompilerParams(
            collective_id=cap, has_side_effects=True, vmem_limit_bytes=60 * 2**20
        ),
        name="attend%d" % cap,
    )(table, own, use, qt, pages, fresh, prefix)


def body(queries, new_kv, kv_pages, page_owner, page_request, page_fill, prefix_kv, prefix_use):
    request_count, step_count, query_width = queries.shape
    smem = pl.BlockSpec(memory_space=pltpu.SMEM)
    vmem = pl.BlockSpec(memory_space=pltpu.VMEM)
    dma = pltpu.SemaphoreType.DMA
    table, own, level = pl.pallas_call(
        meta_kernel,
        out_shape=[
            jax.ShapeDtypeStruct((NCTX, 1, 128), jnp.int32),
            jax.ShapeDtypeStruct((4, 128), jnp.int32),
            jax.ShapeDtypeStruct((1, 128), jnp.int32),
        ],
        in_specs=[smem] * 3,
        out_specs=[vmem] * 3,
        scratch_shapes=[
            pltpu.VMEM((1, 1, 128), jnp.int32),
            pltpu.VMEM((NDP, 8, 128), jnp.int32),
            dma((NDP,)), dma((NDP,)), dma((NCTX,)), dma((NCTX,)),
        ],
        compiler_params=pltpu.CompilerParams(collective_id=0, has_side_effects=True),
        name="meta",
    )(page_owner, page_request, page_fill)

    qt = queries.reshape(request_count, step_count, KVH * G, HD).transpose(0, 3, 2, 1).reshape(request_count, HD, 256)
    fresh = jnp.pad(new_kv, ((0, 0), (0, 12), (0, 0)))
    prefix = prefix_kv.reshape(32, 128)
    out = lax.switch(
        level[0, 0],
        [functools.partial(attend_all, cap) for cap in (1, 2, 4)],
        table, own, prefix_use, qt, kv_pages, fresh, prefix,
    )
    out = out.reshape(request_count, HD, KVH * G, step_count).transpose(0, 3, 2, 1)
    return out.reshape(request_count, step_count, query_width)


def solution(mesh):
    placed = (
        P(("ctx", "dp"), None, None),
        P(("ctx", "dp"), None, None),
        P(("ctx", "dp"), None, None),
        P(("ctx", "dp"), None),
        P(("ctx", "dp")),
        P(("ctx", "dp")),
        P(("ctx", "dp"), None),
        P(("ctx", "dp")),
    )
    return jax.shard_map(
        body, mesh=mesh, in_specs=placed, out_specs=P(("ctx", "dp"), None, None), check_vma=False
    )
```

```python
import functools
import math

import jax
import jax.numpy as jnp
from jax import lax
from jax.experimental import pallas as pl
from jax.experimental.pallas import tpu as pltpu
from jax.sharding import PartitionSpec as P

KVH = 8
HD = 128
G = 8
LOW = -1e30
NY, NZ = 4, 8
NCTX = NY * NZ
NDP = 8
EARLY = 32
RELAY = 12
TAKEN = 20
MESH = pl.DeviceIdType.MESH
SCALE = 1.0 / math.sqrt(HD)


def meta_kernel(
    owner, request, fill, q_ref, prefix_ref,
    table, own, level, qt_ref, rows_ref,
    tally, wide, sa, ra, sb, rb, sc, rc,
):
    me = lax.axis_index("ctx")
    col = lax.axis_index("dp")
    y, z = me // NZ, me % NZ

    def near(i):
        return y * NZ + (z + i) % NZ

    def across(i):
        return ((y + i) % NY) * NZ + z

    barrier = pltpu.get_barrier_semaphore()
    for i in range(1, NDP):
        pl.semaphore_signal(barrier, inc=1, device_id={"dp": (col + i) % NDP}, device_id_type=MESH)
    for i in range(1, NZ):
        pl.semaphore_signal(barrier, inc=1, device_id={"ctx": near(i)}, device_id_type=MESH)
    for i in range(1, NY):
        pl.semaphore_signal(barrier, inc=1, device_id={"ctx": across(i)}, device_id_type=MESH)

    lane = lax.broadcasted_iota(jnp.int32, (8, 128), 1)
    count = jnp.zeros((8, 128), jnp.int32)
    r0 = jnp.full((8, 128), -1, jnp.int32)
    r1, p0, p1, f0, f1 = r0, count, count, count + 1, count + 1
    for p in range(owner.shape[0]):
        hit = lane == owner[p]
        first, second = hit & (count == 0), hit & (count == 1)
        r0, r1 = jnp.where(first, request[p], r0), jnp.where(second, request[p], r1)
        p0, p1 = jnp.where(first, p, p0), jnp.where(second, p, p1)
        f0, f1 = jnp.where(first, fill[p], f0), jnp.where(second, fill[p], f1)
        count = count + hit.astype(jnp.int32)
    extra = jnp.where(count == 2, 1, 0)
    whole = extra
    for k in range(1, NY):
        whole = whole + pltpu.roll(extra, k * NZ, 1)
    tally[0] = jnp.broadcast_to(jnp.max(whole, axis=1, keepdims=True), (8, 128))

    pl.semaphore_wait(barrier, NDP + NZ + NY - 3)

    def tally_copy(i):
        return pltpu.make_async_remote_copy(
            src_ref=tally.at[0], dst_ref=tally.at[i], send_sem=sa.at[i], recv_sem=ra.at[i],
            device_id={"dp": (col + i) % NDP}, device_id_type=MESH)

    for i in range(1, NDP):
        tally_copy(i).start()

    own[0:1, :] = p0[0:1]
    own[1:2, :] = p1[0:1]
    own[2:3, :] = f0[0:1]
    own[3:4, :] = f1[0:1]

    def turn(lo, hi):
        def one(r, c):
            for h in range(2):
                x = q_ref[r, :, pl.ds(h * 4096, 4096)].astype(jnp.float32)
                x = jnp.concatenate([x[:, k * 128:(k + 1) * 128] for k in range(32)], axis=0)
                qt_ref[r, :, pl.ds(h * 128, 128)] = x.T.astype(jnp.bfloat16)
            return c

        lax.fori_loop(lo, hi, one, 0)

    turn(0, 5)
    for i in range(1, NDP):
        tally_copy(i).wait()
    most = tally[0]
    for i in range(1, NDP):
        most = jnp.maximum(most, tally[i])
    row = jnp.where(lane < NCTX, r0, jnp.where(lane < 2 * NCTX, pltpu.roll(r1, NCTX, 1), most))
    table[pl.ds(me, 1)] = row[0:1].reshape(1, 1, 128)

    def row_copy(i):
        return pltpu.make_async_remote_copy(
            src_ref=table.at[me], dst_ref=table.at[me], send_sem=sb.at[i], recv_sem=rb.at[i],
            device_id={"ctx": near(i)}, device_id_type=MESH)

    for i in range(1, NZ):
        row_copy(i).start()
    turn(5, 11)
    x = prefix_ref[...].astype(jnp.float32)
    for t in range(2):
        for c in range(16):
            wide[pl.ds(t * 16 + c, 1), :] = x[t:t + 1, c * 128:(c + 1) * 128]
    rows_ref[...] = wide[...].astype(jnp.bfloat16)
    for i in range(1, NZ):
        row_copy(i).wait()

    def line_copy(i):
        line = table.at[pl.ds(y * NZ, NZ)]
        return pltpu.make_async_remote_copy(
            src_ref=line, dst_ref=line, send_sem=sc.at[i], recv_sem=rc.at[i],
            device_id={"ctx": across(i)}, device_id_type=MESH)

    for i in range(1, NY):
        line_copy(i).start()
    turn(11, 16)
    for i in range(1, NY):
        line_copy(i).wait()
    far = table[0]
    for h in range(1, NCTX):
        far = jnp.maximum(far, table[h])
    need = jnp.max(jnp.where(lax.broadcasted_iota(jnp.int32, (1, 128), 1) >= 2 * NCTX, far, 0), axis=1, keepdims=True)
    level[...] = jnp.broadcast_to(jnp.where(need <= 1, 0, jnp.where(need <= 2, 1, 2)), (1, 128))


def lane_head(rows):
    return lax.broadcasted_iota(jnp.int32, (rows, 128), 1) // 32


def spread(block, rows):
    head = lane_head(rows)
    zero = jnp.zeros_like(block)
    return jnp.concatenate([jnp.where(head == k, block, zero) for k in range(4)], axis=0)


def values_half(values, w):
    stacked = jnp.concatenate(values, axis=0)
    return lax.dot_general(
        stacked, spread(w, w.shape[0]), (((0,), (0,)), ((), ())), preferred_element_type=jnp.float32
    )


def group_half(keys, values, qt, visible):
    s = lax.dot_general(
        keys, spread(qt, HD), (((1,), (0,)), ((), ())), preferred_element_type=jnp.float32
    ) * SCALE
    s = jnp.where(visible, s, LOW)
    m = jnp.max(s, axis=0, keepdims=True)
    w = jnp.where(visible, jnp.exp(s - m), 0.0).astype(jnp.bfloat16)
    l = jnp.sum(w.astype(jnp.float32), axis=0, keepdims=True)
    return m, l, values_half(values, w)


def kernel(
    cap, table, own, use,
    qt_ref, pages_hbm, fresh_ref, prefix_ref,
    out_ref,
    pages_ref, sq, rq, sp, rp, sl, rl,
    sq2, rq2, spk, rpk, sp2, rp2, sl2, rl2, su, ru, sul, rul,
    acc, big, tot, pre0, pre1, pre2, pre3, pre4, new16,
    sq_s, rq_s, sp_s, rp_s, sl_s, rl_s,
    sq2_s, rq2_s, spk_s, rpk_s, sp2_s, rp2_s, sl2_s, rl2_s, su_s, ru_s, sul_s, rul_s,
    a_s, a_r, b_s, b_r, c_s, c_r, page_s,
):
    me = lax.axis_index("ctx")
    col = lax.axis_index("dp")
    y, z = me // NZ, me % NZ

    page_load = pltpu.make_async_copy(pages_hbm, pages_ref, page_s)
    page_load.start()

    def at(a, b):
        return (a % NY) * NZ + b % NZ

    def ahead(i):
        return at(y + i // NZ, z + i % NZ)

    def behind(i):
        return at(y + NY - i // NZ, z + NZ - i % NZ)

    def remote(src, dst, send, recv, ctx):
        return pltpu.make_async_remote_copy(
            src_ref=src, dst_ref=dst, send_sem=send, recv_sem=recv,
            device_id={"ctx": ctx}, device_id_type=MESH)

    def loop(lo, hi, f):
        def step(i, c):
            f(i)
            return c

        lax.fori_loop(lo, hi, step, 0)

    barrier = pltpu.get_barrier_semaphore()
    loop(1, NCTX, lambda i: pl.semaphore_signal(barrier, inc=1, device_id={"ctx": ahead(i)}, device_id_type=MESH))
    loop(1, NDP, lambda i: pl.semaphore_signal(barrier, inc=1, device_id={"dp": (col + i) % NDP}, device_id_type=MESH))
    def wanted(h, second):
        return qt_ref[jnp.maximum(table[h, 0, second * NCTX + me], 0)]

    def second_queries(k):
        i, zh = k // NZ, k % NZ
        sq2[i, zh] = wanted(at(y + i, zh), 1)

    def first_queries(i):
        sq[i] = wanted(ahead(i), 0)

    loop(NZ, NY * NZ, second_queries)
    loop(1, NCTX, first_queries)
    pl.semaphore_wait(barrier, NCTX + NDP - 2)

    def pre_z(i):
        return remote(prefix_ref, pre0.at[i], a_s.at[i], a_r.at[i], at(y, z + i))

    def pre_y(i):
        return remote(pre0, pre1.at[i], b_s.at[i], b_r.at[i], at(y + i, z))

    def pre_dp(i):
        return pltpu.make_async_remote_copy(
            src_ref=pre1, dst_ref=pre2.at[i], send_sem=c_s.at[i], recv_sem=c_r.at[i],
            device_id={"dp": (col + i) % NDP}, device_id_type=MESH)

    loop(1, NZ, lambda i: pre_z(i).start())
    pre0[0] = prefix_ref[...]

    def q2_copy(i):
        return remote(sq2.at[i], rq2.at[i], sq2_s.at[i], rq2_s.at[i], at(y + i, z))

    def q_copy(i):
        return remote(sq.at[i], rq.at[i], sq_s.at[i], rq_s.at[i], ahead(i))

    loop(1, NY, lambda i: q2_copy(i).start())
    loop(1, NCTX, lambda i: q_copy(i).start())
    rq[0] = wanted(me, 0)

    def own_relay(zh):
        rq2[0, zh] = wanted(at(y, zh), 1)

    loop(0, NZ, own_relay)

    loop(1, NZ, lambda i: pre_z(i).wait())
    loop(1, NY, lambda i: pre_y(i).start())
    pre1[0] = pre0[...]

    t = lax.broadcasted_iota(jnp.int32, (16, 128), 0)
    causal = t <= lax.broadcasted_iota(jnp.int32, (16, 128), 1) % 4

    new16[...] = jnp.zeros_like(new16)

    def fresh(r):
        new16[0:4, :] = fresh_ref[r].astype(jnp.float32)
        for h in range(2):
            ln = pl.ds(h * 128, 128)
            keys = new16[:, pl.ds(h * 512, 512)].astype(jnp.bfloat16)
            values = [new16[:, pl.ds(1024 + (4 * h + k) * 128, 128)].astype(jnp.bfloat16) for k in range(4)]
            m, l, o = group_half(keys, values, qt_ref[r, :, ln], causal)
            big[r, :, ln] = m
            tot[r, :, ln] = l
            acc[r, :, ln] = o

    loop(0, 16, fresh)

    page_load.wait()

    def attend(q, p, f, put_o, put_l):
        visible = lax.broadcasted_iota(jnp.int32, (64, 128), 0) < f
        for h in range(2):
            ln = pl.ds(h * 128, 128)
            keys = pages_ref[p, :, pl.ds(h * 512, 512)]
            values = [pages_ref[p, :, pl.ds(1024 + (4 * h + k) * 128, 128)] for k in range(4)]
            m, l, out = group_half(keys, values, q[:, ln], visible)
            put_o[:, ln] = (out * (1.0 / l)).astype(jnp.bfloat16)
            put_l[:, ln] = m + jnp.log(l)

    def p_copy(i):
        return remote(sp.at[i], rp.at[i], sp_s.at[i], rp_s.at[i], behind(i))

    def l_copy(i):
        return remote(sl.at[i], rl.at[i], sl_s.at[i], rl_s.at[i], behind(i))

    def answer(i):
        q_copy(i).wait()
        o = behind(i)
        attend(rq.at[i], own[0, o], own[2, o], sp.at[i], sl.at[i])
        l_copy(i).start()
        p_copy(i).start()

    attend(rq.at[0], own[0, me], own[2, me], rp.at[0], rl.at[0])

    def in_use(h, plane):
        return [(table[h, 0, NCTX + k * NZ + plane] >= 0).astype(jnp.int32) for k in range(NY)]

    def nth(flags, j):
        place, seen = 0, 0
        for k in range(NY):
            place = jnp.where((flags[k] == 1) & (seen == j), k, place)
            seen = seen + flags[k]
        return place

    def pack_copy(d):
        return remote(spk.at[d], rpk.at[d], spk_s.at[d], rpk_s.at[d], at(y, z + d))

    def pack(d, dst):
        zh = (z + d) % NZ
        flags = in_use(at(y, zh), z)
        for j in range(cap):
            dst[d, j] = rq2[(y + NY - nth(flags, j)) % NY, zh]

    def pack_send(d):
        pack(d, spk)
        pack_copy(d).start()

    def p2_copy(d):
        return remote(sp2.at[d], rp2.at[d], sp2_s.at[d], rp2_s.at[d], at(y, z + NZ - d))

    def l2_copy(d):
        return remote(sl2.at[d], rl2.at[d], sl2_s.at[d], rl2_s.at[d], at(y, z + NZ - d))

    def attend2(d, dst_o, dst_l):
        plane = (z + NZ - d) % NZ
        flags = in_use(me, plane)
        for j in range(cap):
            o = nth(flags, j) * NZ + plane
            attend(rpk.at[d, j], own[1, o], own[3, o], dst_o.at[d, j], dst_l.at[d, j])

    def answer2(d):
        pack_copy(d).wait()
        attend2(d, sp2, sl2)
        l2_copy(d).start()
        p2_copy(d).start()

    def u_copy(i, zh):
        return remote(su.at[i, zh], ru.at[i, zh], su_s.at[i, zh], ru_s.at[i, zh], at(y + i, z))

    def ul_copy(i):
        return remote(sul.at[i], rul.at[i], sul_s.at[i], rul_s.at[i], at(y + i, z))

    def hand_on(d):
        zh = (z + d) % NZ
        flags = in_use(at(y, zh), z)
        for i in range(NY):
            k = (y + i) % NY
            before = 0
            for k2 in range(NY):
                before = before + jnp.where(k2 < k, flags[k2], 0)
            o, l = rp2[d, 0], rl2[d, 0]
            for j in range(1, cap):
                o, l = jnp.where(before >= j, rp2[d, j], o), jnp.where(before >= j, rl2[d, j], l)
            if i == 0:
                ru[0, zh] = o
                rul[0, zh] = l
            else:
                su[i, zh] = o
                sul[i, zh] = l
                u_copy(i, zh).start()

    loop(1, RELAY, answer)
    loop(1, NY, lambda i: q2_copy(i).wait())
    loop(1, NZ, pack_send)
    loop(1, NY, lambda i: pre_y(i).wait())
    loop(1, NDP, lambda i: pre_dp(i).start())
    pre2[0] = pre1[...]

    pack(0, rpk)
    attend2(0, rp2, rl2)
    loop(RELAY, EARLY, answer)
    loop(1, NZ, answer2)
    loop(EARLY, NCTX, answer)

    loop(1, NDP, lambda i: pre_dp(i).wait())

    def widen(i):
        pre3[...] = pre2[i].astype(jnp.float32).reshape(NCTX * 32, 128)
        for ch in range(16):
            pre4[ch, pl.ds(pl.multiple_of(i * 2 * NCTX, 2 * NCTX), 2 * NCTX), :] = pre3[
                pl.ds(ch, 2 * NCTX, stride=16), :].astype(jnp.bfloat16)

    loop(0, NDP, widen)

    def prefix(r):
        u = use[r] > 0
        for h in range(2):
            ln = pl.ds(h * 128, 128)
            q = qt_ref[r, :, ln]
            head = lane_head(HD)
            s = jnp.zeros((2 * NCTX * NDP, 128), jnp.float32)
            for k in range(4):
                s = s + lax.dot_general(
                    pre4[4 * h + k], jnp.where(head == k, q, jnp.zeros_like(q)),
                    (((1,), (0,)), ((), ())), preferred_element_type=jnp.float32)
            s = s * SCALE
            m = jnp.max(s, axis=0, keepdims=True)
            w = jnp.exp(s - m).astype(jnp.bfloat16)
            l = jnp.sum(w.astype(jnp.float32), axis=0, keepdims=True)
            o = values_half([pre4[8 + 4 * h + k] for k in range(4)], w)
            m = jnp.where(u, m, LOW)
            l = jnp.where(u, l, 0.0)
            o = jnp.where(u, o, 0.0)
            old = big[r, :, ln]
            new = jnp.maximum(old, m)
            a, b = jnp.exp(old - new), jnp.exp(m - new)
            big[r, :, ln] = new
            tot[r, :, ln] = a * tot[r, :, ln] + b * l
            acc[r, :, ln] = a * acc[r, :, ln] + b * o

    loop(0, 16, prefix)

    def merge(items):
        def one(r):
            ls = [jnp.where(q == r, l[...], LOW) for q, l, _ in items]
            old = big[r]
            new = functools.reduce(jnp.maximum, ls, old)
            a = jnp.exp(old - new)
            bs = [jnp.exp(l - new) for l in ls]
            big[r] = new
            tot[r] = functools.reduce(lambda x, b: x + b, bs, a * tot[r])
            more = a * acc[r]
            for b, (_, _, o) in zip(bs, items):
                more = more + b * o[...].astype(jnp.float32)
            acc[r] = more

        loop(0, 16, one)

    def take(k):
        def arrive(i):
            l_copy(i).wait()
            p_copy(i).wait()

        loop(4 * k, 4 * k + 4, arrive)
        merge([(table[ahead(4 * k + n), 0, me], rl.at[4 * k + n], rp.at[4 * k + n]) for n in range(4)])

    def arrive(i):
        l_copy(i).wait()
        p_copy(i).wait()

    loop(1, 4, arrive)
    merge([(table[ahead(n), 0, me], rl.at[n], rp.at[n]) for n in range(4)])
    loop(1, TAKEN // 4, take)

    def relay_back(d):
        l2_copy(d).wait()
        p2_copy(d).wait()
        hand_on(d)

    hand_on(0)
    loop(1, NZ, relay_back)
    loop(1, NY, lambda i: ul_copy(i).start())
    loop(TAKEN // 4, NCTX // 4, take)

    def merge_second(i, zh):
        n = min(4, NZ)
        hs = [zh + j for j in range(n)]
        merge([(table[at(y + NY - i, h), 0, NCTX + me], rul.at[i, h], ru.at[i, h]) for h in hs])

    def take_second(i):
        ul_copy(i).wait()
        loop(0, NZ, lambda zh: u_copy(i, zh).wait())
        loop(0, max(1, NZ // 4), lambda k: merge_second(i, 4 * k))

    loop(0, max(1, NZ // 4), lambda k: merge_second(0, 4 * k))
    loop(1, NY, take_second)

    def finish(r):
        out_ref[r] = (acc[r] * (1.0 / tot[r])).astype(jnp.bfloat16)

    loop(0, 16, finish)


def attend_all(cap, table, own, use, qt, pages, fresh, prefix):
    smem = pl.BlockSpec(memory_space=pltpu.SMEM)
    vmem = pl.BlockSpec(memory_space=pltpu.VMEM)
    dma = pltpu.SemaphoreType.DMA

    def rows(*lead):
        return pltpu.VMEM(lead + (HD, 256), jnp.bfloat16)

    def stats(*lead):
        return pltpu.VMEM(lead + (1, 256), jnp.float32)

    return pl.pallas_call(
        functools.partial(kernel, cap),
        out_shape=jax.ShapeDtypeStruct(qt.shape, jnp.bfloat16),
        in_specs=[smem] * 3 + [vmem, pl.BlockSpec(memory_space=pl.ANY), vmem, vmem],
        out_specs=vmem,
        scratch_shapes=[
            pltpu.VMEM(pages.shape, jnp.bfloat16),
            rows(NCTX), rows(NCTX), rows(NCTX), rows(NCTX), stats(NCTX), stats(NCTX),
            rows(NY, NZ), rows(NY, NZ), rows(NZ, cap), rows(NZ, cap), rows(NZ, cap), rows(NZ, cap),
            stats(NZ, cap), stats(NZ, cap), rows(NY, NZ), rows(NY, NZ), stats(NY, NZ), stats(NY, NZ),
            pltpu.VMEM((16, HD, 256), jnp.float32), stats(16), stats(16),
            pltpu.VMEM((NZ, 32, 128), jnp.bfloat16),
            pltpu.VMEM((NY, NZ, 32, 128), jnp.bfloat16),
            pltpu.VMEM((NDP, NY, NZ, 32, 128), jnp.bfloat16),
            pltpu.VMEM((NCTX * 32, 128), jnp.float32),
            pltpu.VMEM((16, 2 * NCTX * NDP, 128), jnp.bfloat16),
            pltpu.VMEM((16, 2048), jnp.float32),
            dma((NCTX,)), dma((NCTX,)), dma((NCTX,)), dma((NCTX,)), dma((NCTX,)), dma((NCTX,)),
            dma((NY,)), dma((NY,)), dma((NZ,)), dma((NZ,)), dma((NZ,)), dma((NZ,)), dma((NZ,)), dma((NZ,)),
            dma((NY, NZ)), dma((NY, NZ)), dma((NY,)), dma((NY,)),
            dma((NZ,)), dma((NZ,)), dma((NY,)), dma((NY,)), dma((NDP,)), dma((NDP,)), dma,
        ],
        compiler_params=pltpu.CompilerParams(
            collective_id=cap, has_side_effects=True, vmem_limit_bytes=60 * 2**20
        ),
        name="attend%d" % cap,
    )(table, own, use, qt, pages, fresh, prefix)


def body(queries, new_kv, kv_pages, page_owner, page_request, page_fill, prefix_kv, prefix_use):
    request_count, step_count, query_width = queries.shape
    smem = pl.BlockSpec(memory_space=pltpu.SMEM)
    vmem = pl.BlockSpec(memory_space=pltpu.VMEM)
    dma = pltpu.SemaphoreType.DMA
    table, own, level, qt, prefix = pl.pallas_call(
        meta_kernel,
        out_shape=[
            jax.ShapeDtypeStruct((NCTX, 1, 128), jnp.int32),
            jax.ShapeDtypeStruct((4, 128), jnp.int32),
            jax.ShapeDtypeStruct((1, 128), jnp.int32),
            jax.ShapeDtypeStruct((request_count, HD, 256), jnp.bfloat16),
            jax.ShapeDtypeStruct((32, 128), jnp.bfloat16),
        ],
        in_specs=[smem] * 3 + [vmem] * 2,
        out_specs=[vmem] * 5,
        scratch_shapes=[
            pltpu.VMEM((NDP, 8, 128), jnp.int32),
            pltpu.VMEM((32, 128), jnp.float32),
            dma((NDP,)), dma((NDP,)), dma((NZ,)), dma((NZ,)), dma((NY,)), dma((NY,)),
        ],
        compiler_params=pltpu.CompilerParams(
            collective_id=0, has_side_effects=True, vmem_limit_bytes=60 * 2**20
        ),
        name="meta",
    )(page_owner.reshape(-1), page_request, page_fill, queries, prefix_kv)
    out = lax.switch(
        level[0, 0],
        [functools.partial(attend_all, cap) for cap in (1, 2, 4)],
        table, own, prefix_use, qt, kv_pages, new_kv, prefix,
    )
    out = out.reshape(request_count, HD, KVH * G, step_count).transpose(0, 3, 2, 1)
    return out.reshape(request_count, step_count, query_width)


def solution(mesh):
    placed = (
        P(("ctx", "dp"), None, None),
        P(("ctx", "dp"), None, None),
        P(("ctx", "dp"), None, None),
        P(("ctx", "dp"), None),
        P(("ctx", "dp")),
        P(("ctx", "dp")),
        P(("ctx", "dp"), None),
        P(("ctx", "dp")),
    )
    return jax.shard_map(
        body, mesh=mesh, in_specs=placed, out_specs=P(("ctx", "dp"), None, None), check_vma=False
    )
```

```python
import functools
import math

import jax
import jax.numpy as jnp
from jax import lax
from jax.experimental import pallas as pl
from jax.experimental.pallas import tpu as pltpu
from jax.sharding import PartitionSpec as P

KVH = 8
HD = 128
G = 8
LOW = -1e30
NY, NZ = 4, 8
NCTX = NY * NZ
NDP = 8
EARLY = 32
RELAY = 12
TAKEN = 20
MUL = 11
MESH = pl.DeviceIdType.MESH
SCALE = 1.0 / math.sqrt(HD)


def meta_kernel(
    owner, request, fill, q_ref, prefix_ref,
    table, own, level, qt_ref, rows_ref,
    tally, wide, sa, ra, sb, rb, sc, rc,
):
    me = lax.axis_index("ctx")
    col = lax.axis_index("dp")
    y, z = me // NZ, me % NZ

    def near(i):
        return y * NZ + (z + i) % NZ

    def across(i):
        return ((y + i) % NY) * NZ + z

    barrier = pltpu.get_barrier_semaphore()
    for i in range(1, NDP):
        pl.semaphore_signal(barrier, inc=1, device_id={"dp": (col + i) % NDP}, device_id_type=MESH)
    for i in range(1, NZ):
        pl.semaphore_signal(barrier, inc=1, device_id={"ctx": near(i)}, device_id_type=MESH)
    for i in range(1, NY):
        pl.semaphore_signal(barrier, inc=1, device_id={"ctx": across(i)}, device_id_type=MESH)

    lane = lax.broadcasted_iota(jnp.int32, (8, 128), 1)
    count = jnp.zeros((8, 128), jnp.int32)
    r0 = jnp.full((8, 128), -1, jnp.int32)
    r1, p0, p1, f0, f1 = r0, count, count, count + 1, count + 1
    for p in range(owner.shape[0]):
        hit = lane == owner[p]
        first, second = hit & (count == 0), hit & (count == 1)
        r0, r1 = jnp.where(first, request[p], r0), jnp.where(second, request[p], r1)
        p0, p1 = jnp.where(first, p, p0), jnp.where(second, p, p1)
        f0, f1 = jnp.where(first, fill[p], f0), jnp.where(second, fill[p], f1)
        count = count + hit.astype(jnp.int32)
    extra = jnp.where(count == 2, 1, 0)
    whole = extra
    for k in range(1, NY):
        whole = whole + pltpu.roll(extra, k * NZ, 1)
    tally[0] = jnp.broadcast_to(jnp.max(whole, axis=1, keepdims=True), (8, 128))

    pl.semaphore_wait(barrier, NDP + NZ + NY - 3)

    def tally_copy(i):
        return pltpu.make_async_remote_copy(
            src_ref=tally.at[0], dst_ref=tally.at[i], send_sem=sa.at[i], recv_sem=ra.at[i],
            device_id={"dp": (col + i) % NDP}, device_id_type=MESH)

    for i in range(1, NDP):
        tally_copy(i).start()

    own[0:1, :] = p0[0:1]
    own[1:2, :] = p1[0:1]
    own[2:3, :] = f0[0:1]
    own[3:4, :] = f1[0:1]

    def turn(lo, hi):
        def one(r, c):
            for h in range(2):
                x = q_ref[r, :, pl.ds(h * 4096, 4096)].astype(jnp.float32)
                x = jnp.concatenate([x[:, k * 128:(k + 1) * 128] for k in range(32)], axis=0)
                qt_ref[r, :, pl.ds(h * 128, 128)] = x.T.astype(jnp.bfloat16)
            return c

        lax.fori_loop(lo, hi, one, 0)

    turn(0, 5)
    for i in range(1, NDP):
        tally_copy(i).wait()
    most = tally[0]
    for i in range(1, NDP):
        most = jnp.maximum(most, tally[i])
    row = jnp.where(lane < NCTX, r0, jnp.where(lane < 2 * NCTX, pltpu.roll(r1, NCTX, 1), most))
    table[pl.ds(me, 1)] = row[0:1].reshape(1, 1, 128)

    def row_copy(i):
        return pltpu.make_async_remote_copy(
            src_ref=table.at[me], dst_ref=table.at[me], send_sem=sb.at[i], recv_sem=rb.at[i],
            device_id={"ctx": near(i)}, device_id_type=MESH)

    for i in range(1, NZ):
        row_copy(i).start()
    turn(5, 11)
    x = prefix_ref[...].astype(jnp.float32)
    for t in range(2):
        for c in range(16):
            wide[pl.ds(t * 16 + c, 1), :] = x[t:t + 1, c * 128:(c + 1) * 128]
    rows_ref[...] = wide[...].astype(jnp.bfloat16)
    for i in range(1, NZ):
        row_copy(i).wait()

    def line_copy(i):
        line = table.at[pl.ds(y * NZ, NZ)]
        return pltpu.make_async_remote_copy(
            src_ref=line, dst_ref=line, send_sem=sc.at[i], recv_sem=rc.at[i],
            device_id={"ctx": across(i)}, device_id_type=MESH)

    for i in range(1, NY):
        line_copy(i).start()
    turn(11, 16)
    for i in range(1, NY):
        line_copy(i).wait()
    far = table[0]
    for h in range(1, NCTX):
        far = jnp.maximum(far, table[h])
    need = jnp.max(jnp.where(lax.broadcasted_iota(jnp.int32, (1, 128), 1) >= 2 * NCTX, far, 0), axis=1, keepdims=True)
    level[...] = jnp.broadcast_to(jnp.where(need <= 1, 0, jnp.where(need <= 2, 1, 2)), (1, 128))


def lane_head(rows):
    return lax.broadcasted_iota(jnp.int32, (rows, 128), 1) // 32


def spread(block, rows):
    head = lane_head(rows)
    zero = jnp.zeros_like(block)
    return jnp.concatenate([jnp.where(head == k, block, zero) for k in range(4)], axis=0)


def values_half(values, w):
    stacked = jnp.concatenate(values, axis=0)
    return lax.dot_general(
        stacked, spread(w, w.shape[0]), (((0,), (0,)), ((), ())), preferred_element_type=jnp.float32
    )


def group_half(keys, values, qt, visible):
    s = lax.dot_general(
        keys, spread(qt, HD), (((1,), (0,)), ((), ())), preferred_element_type=jnp.float32
    ) * SCALE
    s = jnp.where(visible, s, LOW)
    m = jnp.max(s, axis=0, keepdims=True)
    w = jnp.where(visible, jnp.exp(s - m), 0.0).astype(jnp.bfloat16)
    l = jnp.sum(w.astype(jnp.float32), axis=0, keepdims=True)
    return m, l, values_half(values, w)


def kernel(
    cap, table, own, use,
    qt_ref, pages_hbm, fresh_ref, prefix_ref,
    out_ref,
    pages_ref, sq, rq, sp, rp, sl, rl,
    sq2, rq2, spk, rpk, sp2, rp2, sl2, rl2, su, ru, sul, rul,
    acc, big, tot, pre0, pre1, pre2, pre3, pre4, new16,
    sq_s, rq_s, sp_s, rp_s, sl_s, rl_s,
    sq2_s, rq2_s, spk_s, rpk_s, sp2_s, rp2_s, sl2_s, rl2_s, su_s, ru_s, sul_s, rul_s,
    a_s, a_r, b_s, b_r, c_s, c_r, page_s,
):
    me = lax.axis_index("ctx")
    col = lax.axis_index("dp")
    y, z = me // NZ, me % NZ

    page_load = pltpu.make_async_copy(pages_hbm, pages_ref, page_s)
    page_load.start()

    def at(a, b):
        return (a % NY) * NZ + b % NZ

    def ahead(i):
        return at(y + i // NZ, z + i % NZ)

    def behind(i):
        return at(y + NY - i // NZ, z + NZ - i % NZ)

    def mix(k):
        return (k * MUL) % NCTX

    def remote(src, dst, send, recv, ctx):
        return pltpu.make_async_remote_copy(
            src_ref=src, dst_ref=dst, send_sem=send, recv_sem=recv,
            device_id={"ctx": ctx}, device_id_type=MESH)

    def loop(lo, hi, f):
        def step(i, c):
            f(i)
            return c

        lax.fori_loop(lo, hi, step, 0)

    barrier = pltpu.get_barrier_semaphore()
    loop(1, NCTX, lambda i: pl.semaphore_signal(barrier, inc=1, device_id={"ctx": ahead(i)}, device_id_type=MESH))
    loop(1, NDP, lambda i: pl.semaphore_signal(barrier, inc=1, device_id={"dp": (col + i) % NDP}, device_id_type=MESH))
    def wanted(h, second):
        return qt_ref[jnp.maximum(table[h, 0, second * NCTX + me], 0)]

    def second_queries(k):
        i, zh = k // NZ, k % NZ
        sq2[i, zh] = wanted(at(y + i, zh), 1)

    def first_queries(i):
        sq[i] = wanted(ahead(i), 0)

    loop(NZ, NY * NZ, second_queries)
    loop(1, NCTX, first_queries)
    pl.semaphore_wait(barrier, NCTX + NDP - 2)

    def pre_z(i):
        return remote(prefix_ref, pre0.at[i], a_s.at[i], a_r.at[i], at(y, z + i))

    def pre_y(i):
        return remote(pre0, pre1.at[i], b_s.at[i], b_r.at[i], at(y + i, z))

    def pre_dp(i):
        return pltpu.make_async_remote_copy(
            src_ref=pre1, dst_ref=pre2.at[i], send_sem=c_s.at[i], recv_sem=c_r.at[i],
            device_id={"dp": (col + i) % NDP}, device_id_type=MESH)

    loop(1, NZ, lambda i: pre_z(i).start())
    pre0[0] = prefix_ref[...]

    def q2_copy(i):
        return remote(sq2.at[i], rq2.at[i], sq2_s.at[i], rq2_s.at[i], at(y + i, z))

    def q_copy(i):
        return remote(sq.at[i], rq.at[i], sq_s.at[i], rq_s.at[i], ahead(i))

    loop(1, NY, lambda i: q2_copy(i).start())
    loop(1, NCTX, lambda k: q_copy(mix(k)).start())
    rq[0] = wanted(me, 0)

    def own_relay(zh):
        rq2[0, zh] = wanted(at(y, zh), 1)

    loop(0, NZ, own_relay)

    loop(1, NZ, lambda i: pre_z(i).wait())
    loop(1, NY, lambda i: pre_y(i).start())
    pre1[0] = pre0[...]

    t = lax.broadcasted_iota(jnp.int32, (16, 128), 0)
    causal = t <= lax.broadcasted_iota(jnp.int32, (16, 128), 1) % 4

    new16[...] = jnp.zeros_like(new16)

    def fresh(r):
        new16[0:4, :] = fresh_ref[r].astype(jnp.float32)
        for h in range(2):
            ln = pl.ds(h * 128, 128)
            keys = new16[:, pl.ds(h * 512, 512)].astype(jnp.bfloat16)
            values = [new16[:, pl.ds(1024 + (4 * h + k) * 128, 128)].astype(jnp.bfloat16) for k in range(4)]
            m, l, o = group_half(keys, values, qt_ref[r, :, ln], causal)
            big[r, :, ln] = m
            tot[r, :, ln] = l
            acc[r, :, ln] = o

    loop(0, 16, fresh)

    page_load.wait()

    def attend(q, p, f, put_o, put_l):
        visible = lax.broadcasted_iota(jnp.int32, (64, 128), 0) < f
        for h in range(2):
            ln = pl.ds(h * 128, 128)
            keys = pages_ref[p, :, pl.ds(h * 512, 512)]
            values = [pages_ref[p, :, pl.ds(1024 + (4 * h + k) * 128, 128)] for k in range(4)]
            m, l, out = group_half(keys, values, q[:, ln], visible)
            put_o[:, ln] = (out * (1.0 / l)).astype(jnp.bfloat16)
            put_l[:, ln] = m + jnp.log(l)

    def p_copy(i):
        return remote(sp.at[i], rp.at[i], sp_s.at[i], rp_s.at[i], behind(i))

    def l_copy(i):
        return remote(sl.at[i], rl.at[i], sl_s.at[i], rl_s.at[i], behind(i))

    def answer(i):
        q_copy(i).wait()
        o = behind(i)
        attend(rq.at[i], own[0, o], own[2, o], sp.at[i], sl.at[i])
        l_copy(i).start()
        p_copy(i).start()

    attend(rq.at[0], own[0, me], own[2, me], rp.at[0], rl.at[0])

    def in_use(h, plane):
        return [(table[h, 0, NCTX + k * NZ + plane] >= 0).astype(jnp.int32) for k in range(NY)]

    def nth(flags, j):
        place, seen = 0, 0
        for k in range(NY):
            place = jnp.where((flags[k] == 1) & (seen == j), k, place)
            seen = seen + flags[k]
        return place

    def pack_copy(d):
        return remote(spk.at[d], rpk.at[d], spk_s.at[d], rpk_s.at[d], at(y, z + d))

    def pack(d, dst):
        zh = (z + d) % NZ
        flags = in_use(at(y, zh), z)
        for j in range(cap):
            dst[d, j] = rq2[(y + NY - nth(flags, j)) % NY, zh]

    def pack_send(d):
        pack(d, spk)
        pack_copy(d).start()

    def p2_copy(d):
        return remote(sp2.at[d], rp2.at[d], sp2_s.at[d], rp2_s.at[d], at(y, z + NZ - d))

    def l2_copy(d):
        return remote(sl2.at[d], rl2.at[d], sl2_s.at[d], rl2_s.at[d], at(y, z + NZ - d))

    def attend2(d, dst_o, dst_l):
        plane = (z + NZ - d) % NZ
        flags = in_use(me, plane)
        for j in range(cap):
            o = nth(flags, j) * NZ + plane
            attend(rpk.at[d, j], own[1, o], own[3, o], dst_o.at[d, j], dst_l.at[d, j])

    def answer2(d):
        pack_copy(d).wait()
        attend2(d, sp2, sl2)
        l2_copy(d).start()
        p2_copy(d).start()

    def u_copy(i, zh):
        return remote(su.at[i, zh], ru.at[i, zh], su_s.at[i, zh], ru_s.at[i, zh], at(y + i, z))

    def ul_copy(i, zh):
        return remote(sul.at[i, zh], rul.at[i, zh], sul_s.at[i, zh], rul_s.at[i, zh], at(y + i, z))

    def hand_on(d):
        zh = (z + d) % NZ
        flags = in_use(at(y, zh), z)
        for i in range(NY):
            k = (y + i) % NY
            before = 0
            for k2 in range(NY):
                before = before + jnp.where(k2 < k, flags[k2], 0)
            o, l = rp2[d, 0], rl2[d, 0]
            for j in range(1, cap):
                o, l = jnp.where(before >= j, rp2[d, j], o), jnp.where(before >= j, rl2[d, j], l)
            if i == 0:
                ru[0, zh] = o
                rul[0, zh] = l
            else:
                su[i, zh] = o
                sul[i, zh] = l
                ul_copy(i, zh).start()
                u_copy(i, zh).start()

    loop(1, RELAY, lambda k: answer(mix(k)))
    loop(1, NY, lambda i: q2_copy(i).wait())
    loop(1, NZ, pack_send)
    loop(1, NY, lambda i: pre_y(i).wait())
    loop(1, NDP, lambda i: pre_dp(i).start())
    pre2[0] = pre1[...]

    pack(0, rpk)
    attend2(0, rp2, rl2)
    loop(RELAY, EARLY, lambda k: answer(mix(k)))
    loop(1, NZ, answer2)
    loop(EARLY, NCTX, lambda k: answer(mix(k)))

    loop(1, NDP, lambda i: pre_dp(i).wait())

    def widen(i):
        pre3[...] = pre2[i].astype(jnp.float32).reshape(NCTX * 32, 128)
        for ch in range(16):
            pre4[ch, pl.ds(pl.multiple_of(i * 2 * NCTX, 2 * NCTX), 2 * NCTX), :] = pre3[
                pl.ds(ch, 2 * NCTX, stride=16), :].astype(jnp.bfloat16)

    loop(0, NDP, widen)

    def prefix(r):
        u = use[r] > 0
        for h in range(2):
            ln = pl.ds(h * 128, 128)
            q = qt_ref[r, :, ln]
            head = lane_head(HD)
            s = jnp.zeros((2 * NCTX * NDP, 128), jnp.float32)
            for k in range(4):
                s = s + lax.dot_general(
                    pre4[4 * h + k], jnp.where(head == k, q, jnp.zeros_like(q)),
                    (((1,), (0,)), ((), ())), preferred_element_type=jnp.float32)
            s = s * SCALE
            m = jnp.max(s, axis=0, keepdims=True)
            w = jnp.exp(s - m).astype(jnp.bfloat16)
            l = jnp.sum(w.astype(jnp.float32), axis=0, keepdims=True)
            o = values_half([pre4[8 + 4 * h + k] for k in range(4)], w)
            m = jnp.where(u, m, LOW)
            l = jnp.where(u, l, 0.0)
            o = jnp.where(u, o, 0.0)
            old = big[r, :, ln]
            new = jnp.maximum(old, m)
            a, b = jnp.exp(old - new), jnp.exp(m - new)
            big[r, :, ln] = new
            tot[r, :, ln] = a * tot[r, :, ln] + b * l
            acc[r, :, ln] = a * acc[r, :, ln] + b * o

    loop(0, 16, prefix)

    def merge(items):
        def one(r):
            ls = [jnp.where(q == r, l[...], LOW) for q, l, _ in items]
            old = big[r]
            new = functools.reduce(jnp.maximum, ls, old)
            a = jnp.exp(old - new)
            bs = [jnp.exp(l - new) for l in ls]
            big[r] = new
            tot[r] = functools.reduce(lambda x, b: x + b, bs, a * tot[r])
            more = a * acc[r]
            for b, (_, _, o) in zip(bs, items):
                more = more + b * o[...].astype(jnp.float32)
            acc[r] = more

        loop(0, 16, one)

    def take(k):
        def arrive(k):
            l_copy(mix(k)).wait()
            p_copy(mix(k)).wait()

        loop(4 * k, 4 * k + 4, arrive)
        ins = [mix(4 * k + n) for n in range(4)]
        merge([(table[ahead(i), 0, me], rl.at[i], rp.at[i]) for i in ins])

    def arrive(k):
        l_copy(mix(k)).wait()
        p_copy(mix(k)).wait()

    loop(1, 4, arrive)
    ins = [mix(n) for n in range(4)]
    merge([(table[ahead(i), 0, me], rl.at[i], rp.at[i]) for i in ins])
    loop(1, TAKEN // 4, take)

    def relay_back(d):
        l2_copy(d).wait()
        p2_copy(d).wait()
        hand_on(d)

    def merge_second(d):
        zh = (z + d) % NZ
        for i in range(1, NY):
            ul_copy(i, zh).wait()
            u_copy(i, zh).wait()
        merge([(table[at(y + NY - i, zh), 0, NCTX + me], rul.at[i, zh], ru.at[i, zh]) for i in range(NY)])

    left = NCTX // 4 - TAKEN // 4
    hand_on(0)

    def back_and_take(d):
        relay_back(d)
        take(TAKEN // 4 + d - 1)

    def back_and_merge(d):
        relay_back(d)
        merge_second(d - 1)

    loop(1, 1 + left, back_and_take)
    loop(0, left, merge_second)
    loop(1 + left, NZ, back_and_merge)
    merge_second(NZ - 1)

    def finish(r):
        out_ref[r] = (acc[r] * (1.0 / tot[r])).astype(jnp.bfloat16)

    loop(0, 16, finish)


def attend_all(cap, table, own, use, qt, pages, fresh, prefix):
    smem = pl.BlockSpec(memory_space=pltpu.SMEM)
    vmem = pl.BlockSpec(memory_space=pltpu.VMEM)
    dma = pltpu.SemaphoreType.DMA

    def rows(*lead):
        return pltpu.VMEM(lead + (HD, 256), jnp.bfloat16)

    def stats(*lead):
        return pltpu.VMEM(lead + (1, 256), jnp.float32)

    return pl.pallas_call(
        functools.partial(kernel, cap),
        out_shape=jax.ShapeDtypeStruct(qt.shape, jnp.bfloat16),
        in_specs=[smem] * 3 + [vmem, pl.BlockSpec(memory_space=pl.ANY), vmem, vmem],
        out_specs=vmem,
        scratch_shapes=[
            pltpu.VMEM(pages.shape, jnp.bfloat16),
            rows(NCTX), rows(NCTX), rows(NCTX), rows(NCTX), stats(NCTX), stats(NCTX),
            rows(NY, NZ), rows(NY, NZ), rows(NZ, cap), rows(NZ, cap), rows(NZ, cap), rows(NZ, cap),
            stats(NZ, cap), stats(NZ, cap), rows(NY, NZ), rows(NY, NZ), stats(NY, NZ), stats(NY, NZ),
            pltpu.VMEM((16, HD, 256), jnp.float32), stats(16), stats(16),
            pltpu.VMEM((NZ, 32, 128), jnp.bfloat16),
            pltpu.VMEM((NY, NZ, 32, 128), jnp.bfloat16),
            pltpu.VMEM((NDP, NY, NZ, 32, 128), jnp.bfloat16),
            pltpu.VMEM((NCTX * 32, 128), jnp.float32),
            pltpu.VMEM((16, 2 * NCTX * NDP, 128), jnp.bfloat16),
            pltpu.VMEM((16, 2048), jnp.float32),
            dma((NCTX,)), dma((NCTX,)), dma((NCTX,)), dma((NCTX,)), dma((NCTX,)), dma((NCTX,)),
            dma((NY,)), dma((NY,)), dma((NZ,)), dma((NZ,)), dma((NZ,)), dma((NZ,)), dma((NZ,)), dma((NZ,)),
            dma((NY, NZ)), dma((NY, NZ)), dma((NY, NZ)), dma((NY, NZ)),
            dma((NZ,)), dma((NZ,)), dma((NY,)), dma((NY,)), dma((NDP,)), dma((NDP,)), dma,
        ],
        compiler_params=pltpu.CompilerParams(
            collective_id=cap, has_side_effects=True, vmem_limit_bytes=60 * 2**20
        ),
        name="attend%d" % cap,
    )(table, own, use, qt, pages, fresh, prefix)


def body(queries, new_kv, kv_pages, page_owner, page_request, page_fill, prefix_kv, prefix_use):
    request_count, step_count, query_width = queries.shape
    smem = pl.BlockSpec(memory_space=pltpu.SMEM)
    vmem = pl.BlockSpec(memory_space=pltpu.VMEM)
    dma = pltpu.SemaphoreType.DMA
    table, own, level, qt, prefix = pl.pallas_call(
        meta_kernel,
        out_shape=[
            jax.ShapeDtypeStruct((NCTX, 1, 128), jnp.int32),
            jax.ShapeDtypeStruct((4, 128), jnp.int32),
            jax.ShapeDtypeStruct((1, 128), jnp.int32),
            jax.ShapeDtypeStruct((request_count, HD, 256), jnp.bfloat16),
            jax.ShapeDtypeStruct((32, 128), jnp.bfloat16),
        ],
        in_specs=[smem] * 3 + [vmem] * 2,
        out_specs=[vmem] * 5,
        scratch_shapes=[
            pltpu.VMEM((NDP, 8, 128), jnp.int32),
            pltpu.VMEM((32, 128), jnp.float32),
            dma((NDP,)), dma((NDP,)), dma((NZ,)), dma((NZ,)), dma((NY,)), dma((NY,)),
        ],
        compiler_params=pltpu.CompilerParams(
            collective_id=0, has_side_effects=True, vmem_limit_bytes=60 * 2**20
        ),
        name="meta",
    )(page_owner.reshape(-1), page_request, page_fill, queries, prefix_kv)
    out = lax.switch(
        level[0, 0],
        [functools.partial(attend_all, cap) for cap in (1, 2, 4)],
        table, own, prefix_use, qt, kv_pages, new_kv, prefix,
    )
    out = out.reshape(request_count, HD, KVH * G, step_count).transpose(0, 3, 2, 1)
    return out.reshape(request_count, step_count, query_width)


def solution(mesh):
    placed = (
        P(("ctx", "dp"), None, None),
        P(("ctx", "dp"), None, None),
        P(("ctx", "dp"), None, None),
        P(("ctx", "dp"), None),
        P(("ctx", "dp")),
        P(("ctx", "dp")),
        P(("ctx", "dp"), None),
        P(("ctx", "dp")),
    )
    return jax.shard_map(
        body, mesh=mesh, in_specs=placed, out_specs=P(("ctx", "dp"), None, None), check_vma=False
    )
```
